32 devices in a mesh: grp: 2 (over x), row: 8 (over z, y), col: 2 (over core).
Axes of the slice: x: 2, y: 2, z: 4, core: 2. Of those that a mesh axis runs over, the one named last changes fastest.
Arguments:
- start_block: float32 [128, 1024], P(('grp', 'row', 'col')), parts along dimension 0
- tiles: float32 [8192, 4096], P(('grp', 'row', 'col')), parts along dimension 0, as said below
- tile_rows: int32 [8192], P(('grp', 'row', 'col')), parts along dimension 0, may hold values from 0 to 63, as said below
- tile_cols: int32 [8192], P(('grp', 'row', 'col')), parts along dimension 0, may hold values from 0 to 63, as said below
- counts: int32 [32], P(('grp', 'row', 'col')), parts along dimension 0, may hold values from 85 to 256, as said below
Outputs:
- basis: float32 [128, 1024], P(('grp', 'row', 'col')), parts along dimension 0
- coefficients: float32 [8, 16, 16], P('grp'), parts along dimension 0
The draws below stay inside these ranges and needn't reach their ends.
There are 2 independent parts, one for each index of `grp`. The reference program is written for one: setup_inputs(seed, part) draws one part's arguments, and reference() takes and returns one part's arrays. A program takes and returns all parts, laid end to end along the dimension named above; each array names one. Nothing has to cross between parts.
Inputs may be any that keep to these rules, and one draw needn't show every extreme that they name: Device d = r * 2 + c (r its row index, c its col index) holds slots d * 256 to (d + 1) * 256 - 1; each such slot's tile_rows lies in [r * 2 * 4, (r + 1) * 2 * 4). For the slots of device d = r * 2 + c, tile_cols >= tile_rows and (tile_cols // 4) % 2 == c. Only the first counts[d] slots of device d are live; some device has 256 live slots. `tiles`: entries have row scales that differ from block row to block row.
All inputs are finite; a program needn't handle non-finite values.
Results may differ from the reference program's by a relative error of at most 0.00012.
Values sent between devices are 32-bit elements; how exact they have to be, the bound alone decides.
A program may use at most 64 MiB of HBM per device.

```python
import math
import jax
import jax.numpy as jnp
from jax import lax

BS = 64
K = 16
PB = 4
CAP = 256
ROW_DEVS = 8
COL_DEVS = 2
DEVS = 16
NB = 64
NTOT = 4096


def tile_pattern(key):
    key_row, key_piece, key_offset, key_count, key_full = jax.random.split(key, 5)
    slot_total = DEVS * CAP
    slot_index = jnp.arange(slot_total, dtype=jnp.int32)
    device = slot_index // CAP
    within = slot_index % CAP
    row_group = device // COL_DEVS
    col_group = device % COL_DEVS
    band_start = row_group * COL_DEVS * PB
    row_block = band_start + jax.random.randint(key_row, (slot_total,), 0, (col_group + 1) * PB, dtype=jnp.int32)
    row_block = jnp.where(within == 0, band_start + (col_group + 1) * PB - 1, row_block)
    row_block = jnp.where(within == 1, band_start, row_block)
    row_piece = row_block // PB
    col_piece = jax.random.randint(key_piece, (slot_total,), row_group, ROW_DEVS, dtype=jnp.int32) * COL_DEVS + col_group
    col_piece = jnp.where(within == 0, (ROW_DEVS - 1) * COL_DEVS + col_group, col_piece)
    col_piece = jnp.where(within == 1, row_group * COL_DEVS + col_group, col_piece)
    lowest = jnp.where(col_piece == row_piece, row_block % PB, 0)
    col_block = col_piece * PB + jax.random.randint(key_offset, (slot_total,), lowest, PB, dtype=jnp.int32)
    col_block = jnp.where(within == 0, col_piece * PB + PB - 1, col_block)
    col_block = jnp.where(within == 1, col_piece * PB + lowest, col_block)
    live_counts = jax.random.randint(key_count, (DEVS,), CAP // 3, CAP + 1, dtype=jnp.int32)
    fullest = jax.random.randint(key_full, (), 0, DEVS, dtype=jnp.int32)
    device_ids = jnp.arange(DEVS, dtype=jnp.int32)
    live_counts = jnp.where(device_ids == fullest, CAP, live_counts)
    live_counts = jnp.where(device_ids == (fullest + 1) % DEVS, CAP // 3, live_counts)
    return (row_block, col_block, live_counts)


def row_scales(key, slope, spread):
    position = jnp.arange(NB, dtype=jnp.float32) / max(NB - 1, 1)
    ramp = 1.0 + slope * position
    rough = jnp.exp(jax.random.uniform(key, (NB, BS), jnp.float32, 0.0, math.log(spread)))
    return ramp[:, None] * rough


def draw_tile_rows(key, part):
    return tile_pattern(key)[0]


def draw_tile_cols(key, part):
    return tile_pattern(key)[1]


def draw_counts(key, part):
    return tile_pattern(key)[2]


def draw_tiles(key, part):
    row_block, col_block, unused = tile_pattern(key)
    key = jax.random.fold_in(key, 7)
    key_rough, key_entry = jax.random.split(key)
    scales = row_scales(key_rough, 0.8, 3.2)
    entries = jax.random.normal(key_entry, (DEVS * CAP, BS, BS), jnp.float32)
    sigma = 1.0 / math.sqrt(BS * 4.0 * CAP / (3.0 * PB) * 8.0)
    tile_values = entries * scales[row_block][:, :, None] * scales[col_block][:, None, :] * sigma
    return tile_values.reshape(DEVS * CAP, BS * BS)


def draw_start_block(key, part):
    key = jax.random.fold_in(key, 3)
    key_rough, key_entry = jax.random.split(key)
    scales = row_scales(key_rough, 0.8, 3.2)
    entries = jax.random.normal(key_entry, (NB, K, BS), jnp.float32)
    return (entries * scales[:, None, :]).reshape(NB, K * BS)


def setup_inputs(seed: int = 0, part: int = 0) -> dict:
    streams_of = jax.random.split(jax.random.key(seed), 6)
    own_keys = jax.random.split(jax.random.fold_in(streams_of[5], part), 6)
    start_block = draw_start_block(jax.random.fold_in(jax.random.fold_in(streams_of[5], part), 71), part)
    tiles = draw_tiles(jax.random.fold_in(jax.random.fold_in(streams_of[5], part), 71), part)
    tile_rows = draw_tile_rows(jax.random.fold_in(jax.random.fold_in(streams_of[5], part), 71), part)
    tile_cols = draw_tile_cols(jax.random.fold_in(jax.random.fold_in(streams_of[5], part), 71), part)
    counts = draw_counts(jax.random.fold_in(jax.random.fold_in(streams_of[5], part), 71), part)
    return dict(start_block=start_block, tiles=tiles, tile_rows=tile_rows, tile_cols=tile_cols, counts=counts)


highest = lax.Precision.HIGHEST

def gram_of(left_block, right_block):
    return jnp.einsum('jkb,jlb->kl', left_block, right_block, precision=highest)

def mix(matrix, stacked):
    return jnp.einsum('lk,jlb->jkb', matrix, stacked, precision=highest)

def factor(gram_matrix):
    lower_factor = jnp.linalg.cholesky(gram_matrix)
    identity = jnp.eye(gram_matrix.shape[0], dtype=gram_matrix.dtype)
    inverse_factor = lax.linalg.triangular_solve(lower_factor, identity, left_side=True, lower=True)
    return (lower_factor, inverse_factor)

def operate(stacked, tile_stack, row_table, col_table, alive_table):
    block_count = stacked.shape[0]

    def visit(running, scan_item):
        tile_group, row_index, col_index, alive_mask = scan_item
        source_rows = stacked[row_index]
        source_cols = stacked[col_index]
        front = jnp.einsum('cab,ckb->cka', tile_group, source_cols, precision=highest) * alive_mask[:, None, None]
        back = jnp.einsum('cab,cka->ckb', tile_group, source_rows, precision=highest) * alive_mask[:, None, None]
        running = running + jax.ops.segment_sum(front, row_index, block_count) + jax.ops.segment_sum(back, col_index, block_count)
        return (running, None)
    initial = jnp.zeros((block_count, K, BS), dtype=stacked.dtype)
    result, unused = lax.scan(visit, initial, (tile_stack, row_table, col_table, alive_table))
    return result

def reference(start_block, tiles, tile_rows, tile_cols, counts):
    total_rows = NTOT
    start = start_block.reshape(NB, K, BS)
    tile_stack = tiles.reshape(DEVS, CAP, BS, BS)
    row_table = tile_rows.reshape(DEVS, CAP).astype(jnp.int32)
    col_table = tile_cols.reshape(DEVS, CAP).astype(jnp.int32)
    alive_table = (jnp.arange(CAP, dtype=jnp.int32)[None, :] < counts[:, None]).astype(tiles.dtype)

    def apply_matrix(stacked):
        return operate(stacked, tile_stack, row_table, col_table, alive_table)
    unused_factor, inverse_start = factor(gram_of(start, start) / total_rows)
    first_basis = mix(inverse_start.T, start)
    product_block = apply_matrix(first_basis)
    first_proj = gram_of(first_basis, product_block) / total_rows
    residual = product_block - mix(first_proj, first_basis)
    first_lower, first_inverse = factor(gram_of(residual, residual) / total_rows)
    second_basis = mix(first_inverse.T, residual)
    product_block = apply_matrix(second_basis) - mix(first_lower, first_basis)
    second_proj = gram_of(second_basis, product_block) / total_rows
    residual = product_block - mix(second_proj, second_basis)
    second_lower, second_inverse = factor(gram_of(residual, residual) / total_rows)
    third_basis = mix(second_inverse.T, residual)
    return (third_basis.reshape(NB, K * BS), jnp.stack([first_proj, first_lower, second_proj, second_lower]))
```

```python
import functools

import jax
import jax.numpy as jnp
from jax import lax
from jax.experimental import pallas as pl
from jax.experimental.pallas import tpu as pltpu
from jax.sharding import PartitionSpec as P

BS = 64
K = 16
F32 = jnp.float32
BF16 = jnp.bfloat16
MESH = pl.DeviceIdType.MESH
HIGHEST = lax.Precision.HIGHEST


def dot_nn(a, b):
    precision = HIGHEST if a.dtype == F32 else None
    return lax.dot_general(a, b, (((1,), (0,)), ((), ())), precision=precision, preferred_element_type=F32)


def dot_nt(a, b):
    precision = HIGHEST if a.dtype == F32 else None
    return lax.dot_general(a, b, (((1,), (1,)), ((), ())), precision=precision, preferred_element_type=F32)


def split2(x):
    high = x.astype(BF16)
    return high, (x - high.astype(F32)).astype(BF16)


def split3(x):
    high = x.astype(BF16)
    rest = x - high.astype(F32)
    middle = rest.astype(BF16)
    return high, middle, (rest - middle.astype(F32)).astype(BF16)


def factor(gram):
    row = lax.broadcasted_iota(jnp.int32, (K, K), 0)
    col = lax.broadcasted_iota(jnp.int32, (K, K), 1)
    upper = gram
    inverse = (row == col).astype(F32)
    for j in range(K):
        ratio = upper[:, j : j + 1] / upper[j : j + 1, j : j + 1]
        ratio = jnp.where(row > j, jnp.broadcast_to(ratio, (K, K)), 0.0)
        upper, inverse = upper - ratio * upper[j : j + 1, :], inverse - ratio * inverse[j : j + 1, :]
    diagonal = jnp.sum(jnp.where(row == col, upper, 0.0), axis=1, keepdims=True)
    scale = 1.0 / jnp.sqrt(diagonal)
    return jnp.where(col >= row, upper * scale, 0.0), inverse * scale


def kernel(
    rows_n, cols_n, pb,
    start, tiles, tile_rows, tile_cols, counts, basis, coef,
    f0, f1, f2, fq1, fw, fq2, dh, dl, lext, permt, chunk, piece, fb, sb, rs, rsib, acc,
    ags, agf, agr, rss, rsr, sibs, sibr,
):
    r = lax.axis_index("row")
    c = lax.axis_index("col")
    other = 1 - c
    piece_lanes = pb * BS
    total = float(rows_n * cols_n * piece_lanes)
    row_blocks = cols_n * pb
    row_lanes = row_blocks * BS
    pairs = BS // 2

    barrier = pltpu.get_barrier_semaphore()
    pl.semaphore_signal(barrier, inc=1, device_id={"row": r, "col": other}, device_id_type=MESH)
    for i in range(1, rows_n):
        pl.semaphore_signal(
            barrier, inc=1, device_id={"row": lax.rem(r + i, rows_n), "col": c}, device_id_type=MESH
        )

    lane = lax.broadcasted_iota(jnp.int32, (8, 128), 1)

    def lanes_of(col, row):
        return pl.ds(pl.multiple_of((col * rows_n + row) * piece_lanes, 128), piece_lanes)

    own = lanes_of(c, r)

    for j in range(pb):
        for m in range(K // 2):
            chunk[j * 8 + m : j * 8 + m + 1, :] = start[j : j + 1, m * 128 : (m + 1) * 128]
    for jp in range(pb // 2):
        one = chunk[jp * 16 : jp * 16 + 8, :]
        two = chunk[jp * 16 + 8 : jp * 16 + 16, :]
        piece[jp, pl.ds(0, 8, stride=2), :] = jnp.where(
            lane < 64, one, pltpu.roll(two, 64, 1)
        )
        piece[jp, pl.ds(1, 8, stride=2), :] = jnp.where(
            lane < 64, pltpu.roll(one, 64, 1), two
        )
    f0[:, own] = jnp.concatenate([piece[jp] for jp in range(pb // 2)], axis=1)

    def ag_copy(ref, ph, col, row, send_sem, target_row, target_col):
        return pltpu.make_async_remote_copy(
            src_ref=ref.at[:, lanes_of(col, row)],
            dst_ref=ref.at[:, lanes_of(col, row)],
            send_sem=send_sem,
            recv_sem=agr.at[ph, col, row],
            device_id={"row": target_row, "col": target_col},
            device_id_type=MESH,
        )

    def ag_start(ref, ph):
        for i in range(rows_n - 1, 0, -1):
            ag_copy(ref, ph, c, r, ags.at[ph, i], lax.rem(r + i, rows_n), c).start()
        ag_copy(ref, ph, c, r, ags.at[ph, 0], r, other).start()

    def ag_forward(ref, ph):
        for i in range(1, rows_n):
            source = lax.rem(r + i, rows_n)
            copy = ag_copy(ref, ph, c, source, agf.at[ph, i], r, other)
            copy.wait_recv()
            copy.start()

    def ag_end(ref, ph):
        for i in range(rows_n):
            source = lax.rem(r + i, rows_n)
            ag_copy(ref, ph, other, source, agf.at[ph, i], r, other).wait_recv()

    def ag_drain(ref, ph):
        for i in range(1, rows_n):
            ag_copy(ref, ph, c, r, ags.at[ph, i], lax.rem(r + i, rows_n), c).wait_send()
            ag_copy(ref, ph, c, lax.rem(r + i, rows_n), agf.at[ph, i], r, other).wait_send()
        ag_copy(ref, ph, c, r, ags.at[ph, 0], r, other).wait_send()

    def rs_copy(ph, source, target):
        return pltpu.make_async_remote_copy(
            src_ref=sb.at[ph, target],
            dst_ref=rs.at[ph, source],
            send_sem=rss.at[ph, target],
            recv_sem=rsr.at[ph, source],
            device_id={"row": target, "col": c},
            device_id_type=MESH,
        )

    def half(col):
        return pl.ds(pl.multiple_of(col * piece_lanes, 128), piece_lanes)

    def sib_copy(ph):
        return pltpu.make_async_remote_copy(
            src_ref=fb.at[ph, :, half(other)],
            dst_ref=rsib.at[ph],
            send_sem=sibs.at[ph],
            recv_sem=sibr.at[ph],
            device_id={"row": r, "col": other},
            device_id_type=MESH,
        )

    pl.semaphore_wait(barrier, rows_n)
    ag_start(f0, 0)

    q = lax.broadcasted_iota(jnp.int32, (row_blocks * pairs, row_lanes), 0)
    p = lax.broadcasted_iota(jnp.int32, (row_blocks * pairs, row_lanes), 1)
    place = (q % row_blocks) * BS + (q // row_blocks) * 2
    permt[0] = (p == place).astype(F32).astype(BF16)
    permt[1] = (p == place + 1).astype(F32).astype(BF16)

    slots = tile_rows.shape[1]
    places = rows_n * pb * row_blocks
    tr = tile_rows[...]
    tc = tile_cols[...]
    position = (
        ((tc // (pb * cols_n)) * pb + tc % pb) * row_blocks + (tr - r * row_blocks)
    )
    slot = lax.broadcasted_iota(jnp.int32, (1, slots), 1)
    position = jnp.where(slot < counts[0], position, -1)
    pick = (lax.broadcasted_iota(jnp.int32, (places, slots), 0) == position).astype(F32).astype(BF16)

    def densify(i, carry):
        high, low = split2(tiles[:, pl.ds(pl.multiple_of(i * 256, 256), 256)])
        x = dot_nn(pick, high) + dot_nn(pick, low)
        for j in range(rows_n * pb):
            block = x[j * 8 : (j + 1) * 8]
            high, low = split2(jnp.concatenate([block[:, :128], block[:, 128:]], axis=0))
            at = pl.ds(pl.multiple_of(i * 16, 16), 16)
            dh[at, j * 128 : (j + 1) * 128] = high
            dl[at, j * 128 : (j + 1) * 128] = low
        return carry

    lax.fori_loop(0, pairs // 2, densify, 0)

    def product(ref, ph):
        across = jnp.concatenate([ref[:, lanes_of(i, r)] for i in range(cols_n)], axis=1)
        parts = jnp.concatenate(split3(across), axis=0)
        even = dot_nt(parts, permt[0]).astype(BF16)
        odd = dot_nt(parts, permt[1]).astype(BF16)
        lrow = jnp.concatenate(
            [x[i * K : (i + 1) * K] for i in range(3) for x in (even, odd)], axis=0
        )
        wide = lax.broadcasted_iota(jnp.int32, (K, 128), 1)
        low_half = wide < 64

        def back(step, carry):
            target = rows_n - 1 - step
            at = pl.ds(pl.multiple_of(target * pb * 128, 128), pb * 128)
            v = ref[:, lanes_of(c, target)]
            extended = []
            for jp in range(pb // 2):
                x = v[:, jp * 128 : (jp + 1) * 128]
                y = pltpu.roll(x, 64, 1)
                extended.append(
                    jnp.concatenate([jnp.where(low_half, x, 0.0), jnp.where(low_half, 0.0, y)], axis=0)
                )
                extended.append(
                    jnp.concatenate([jnp.where(low_half, y, 0.0), jnp.where(low_half, 0.0, x)], axis=0)
                )
            lext[:, at] = jnp.concatenate(split3(jnp.concatenate(extended, axis=1)), axis=0)

            @pl.when(target >= r)
            def _():
                x = dot_nn(lrow, dh[:, at])
                y = dot_nn(lrow[: 4 * K], dl[:, at])
                z = x[4 * K :] + (x[2 * K : 4 * K] + y[2 * K :]) + y[: 2 * K] + x[: 2 * K]
                sums = []
                for j in range(pb):
                    s = jnp.where(
                        low_half, z[:K, j * 128 : (j + 1) * 128], z[K:, j * 128 : (j + 1) * 128]
                    )
                    sums.append(s + pltpu.roll(s, 64, 1))
                sb[ph, target] = jnp.concatenate(
                    [jnp.where(low_half, sums[2 * j], sums[2 * j + 1]) for j in range(pb // 2)], axis=1
                )

            @pl.when(target > r)
            def _():
                rs_copy(ph, r, target).start()

            return carry

        lax.fori_loop(0, rows_n, back, 0)

        x = dot_nt(lext[...], dh[...])
        y = dot_nt(lext[: 4 * K, :], dl[...])
        z = x[4 * K :] + (x[2 * K : 4 * K] + y[2 * K :]) + y[: 2 * K] + x[: 2 * K]
        parts = split3(z)
        out = dot_nn(jnp.concatenate([x[:K] for x in parts], axis=0), permt[0]) + dot_nn(
            jnp.concatenate([x[K:] for x in parts], axis=0), permt[1]
        )
        fb[ph] = out[2 * K :] + out[K : 2 * K] + out[:K]
        sib_copy(ph).start()

    def collect(ph):
        acc[...] = sb[ph, r] + fb[ph, :, half(c)]

        def add(source, carry):
            @pl.when(source < r)
            def _():
                rs_copy(ph, source, r).wait_recv()
                acc[...] += rs[ph, source]

            return carry

        lax.fori_loop(0, rows_n, add, 0)
        sib_copy(ph).wait_recv()
        return acc[...] + rsib[ph]

    def rs_drain(ph):
        def step(target, carry):
            @pl.when(target > r)
            def _():
                rs_copy(ph, r, target).wait_send()

            return carry

        lax.fori_loop(0, rows_n, step, 0)
        sib_copy(ph).wait_send()

    identity = (
        lax.broadcasted_iota(jnp.int32, (K, K), 0) == lax.broadcasted_iota(jnp.int32, (K, K), 1)
    ).astype(F32)

    ag_forward(f0, 0)
    ag_end(f0, 0)
    product(f0, 0)
    v = f0[...]
    unused, inverse0 = factor(dot_nt(v, v) / total)
    fq1[...] = dot_nn(inverse0, v)

    f1[:, own] = collect(0)
    ag_start(f1, 1)
    ag_forward(f1, 1)
    ag_end(f1, 1)
    z1 = dot_nn(inverse0, f1[...])
    q1 = fq1[...]
    a1 = dot_nt(q1, z1) / total
    coef[0] = a1
    fw[...] = z1 - dot_nn(a1.T, q1)
    product(fw, 1)
    w1 = fw[...]
    upper1, inverse1 = factor(dot_nt(w1, w1) / total)
    coef[1] = dot_nt(identity, upper1)
    fq2[...] = dot_nn(inverse1, w1)
    behind = dot_nn(upper1, fq1[:, own])

    f2[:, own] = dot_nn(inverse1, collect(1)) - behind
    ag_start(f2, 2)
    ag_forward(f2, 2)
    ag_end(f2, 2)
    z2 = f2[...]
    q2 = fq2[...]
    a2 = dot_nt(q2, z2) / total
    coef[2] = a2
    a2t = a2.T
    w2 = z2 - dot_nn(a2t, q2)
    upper2, inverse2 = factor(dot_nt(w2, w2) / total)
    coef[3] = dot_nt(identity, upper2)
    piece_out = dot_nn(inverse2, f2[:, own] - dot_nn(a2t, fq2[:, own]))
    for jp in range(pb // 2):
        piece[jp] = piece_out[:, jp * 128 : (jp + 1) * 128]
    for jp in range(pb // 2):
        one = piece[jp, pl.ds(0, 8, stride=2), :]
        two = piece[jp, pl.ds(1, 8, stride=2), :]
        chunk[jp * 16 : jp * 16 + 8, :] = jnp.where(lane < 64, one, pltpu.roll(two, 64, 1))
        chunk[jp * 16 + 8 : jp * 16 + 16, :] = jnp.where(lane < 64, pltpu.roll(one, 64, 1), two)
    for j in range(pb):
        for m in range(K // 2):
            basis[j : j + 1, m * 128 : (m + 1) * 128] = chunk[j * 8 + m : j * 8 + m + 1, :]

    for ph, ref in enumerate((f0, f1, f2)):
        ag_drain(ref, ph)
    for ph in range(2):
        rs_drain(ph)


def solution(mesh):
    rows_n = mesh.shape["row"]
    cols_n = mesh.shape["col"]

    def per_device(start_block, tiles, tile_rows, tile_cols, counts):
        pb = start_block.shape[0]
        slots = tile_rows.shape[0]
        length = rows_n * cols_n * pb * BS
        wide = rows_n * pb * 128
        tall = cols_n * pb * BS // 2
        vmem = pl.BlockSpec(memory_space=pltpu.VMEM)
        return pl.pallas_call(
            functools.partial(kernel, rows_n, cols_n, pb),
            out_shape=(
                jax.ShapeDtypeStruct(start_block.shape, F32),
                jax.ShapeDtypeStruct((4, K, K), F32),
            ),
            in_specs=[vmem] * 4 + [pl.BlockSpec(memory_space=pltpu.SMEM)],
            out_specs=(vmem, vmem),
            scratch_shapes=[pltpu.VMEM((K, length), F32)] * 6
            + [
                pltpu.VMEM((tall, wide), BF16),
                pltpu.VMEM((tall, wide), BF16),
                pltpu.VMEM((6 * K, wide), BF16),
                pltpu.VMEM((2, tall, 2 * tall), BF16),
                pltpu.VMEM((pb * K // 2, 128), F32),
                pltpu.VMEM((pb // 2, K, 128), F32),
                pltpu.VMEM((2, K, cols_n * pb * BS), F32),
                pltpu.VMEM((2, rows_n, K, pb * BS), F32),
                pltpu.VMEM((2, rows_n, K, pb * BS), F32),
                pltpu.VMEM((2, K, pb * BS), F32),
                pltpu.VMEM((K, pb * BS), F32),
                pltpu.SemaphoreType.DMA((3, rows_n)),
                pltpu.SemaphoreType.DMA((3, rows_n)),
                pltpu.SemaphoreType.DMA((3, cols_n, rows_n)),
                pltpu.SemaphoreType.DMA((2, rows_n)),
                pltpu.SemaphoreType.DMA((2, rows_n)),
                pltpu.SemaphoreType.DMA((2,)),
                pltpu.SemaphoreType.DMA((2,)),
            ],
            compiler_params=pltpu.CompilerParams(
                collective_id=0, has_side_effects=True, vmem_limit_bytes=56 * 2**20
            ),
        )(
            start_block,
            tiles,
            tile_rows.reshape(1, slots),
            tile_cols.reshape(1, slots),
            counts,
        )

    return jax.shard_map(
        per_device,
        mesh=mesh,
        in_specs=(
            P(("grp", "row", "col"), None),
            P(("grp", "row", "col"), None),
            P(("grp", "row", "col")),
            P(("grp", "row", "col")),
            P(("grp", "row", "col")),
        ),
        out_specs=(P(("grp", "row", "col"), None), P("grp", None, None)),
        check_vma=False,
    )
```

```python
import functools

import jax
import jax.numpy as jnp
from jax import lax
from jax.experimental import pallas as pl
from jax.experimental.pallas import tpu as pltpu
from jax.sharding import PartitionSpec as P

BS = 64
K = 16
F32 = jnp.float32
BF16 = jnp.bfloat16
MESH = pl.DeviceIdType.MESH
HIGHEST = lax.Precision.HIGHEST


def dot_nn(a, b):
    precision = HIGHEST if a.dtype == F32 else None
    return lax.dot_general(a, b, (((1,), (0,)), ((), ())), precision=precision, preferred_element_type=F32)


def dot_nt(a, b):
    precision = HIGHEST if a.dtype == F32 else None
    return lax.dot_general(a, b, (((1,), (1,)), ((), ())), precision=precision, preferred_element_type=F32)


def split2(x):
    high = x.astype(BF16)
    return high, (x - high.astype(F32)).astype(BF16)


def split3(x):
    high = x.astype(BF16)
    rest = x - high.astype(F32)
    middle = rest.astype(BF16)
    return high, middle, (rest - middle.astype(F32)).astype(BF16)


def parts_of(x):
    return jnp.concatenate(split3(x), axis=0)


def gram_of(left, right):
    m = dot_nt(left, right)
    m = m[2 * K :] + m[K : 2 * K] + m[:K]
    return m[:, 2 * K :] + m[:, K : 2 * K] + m[:, :K]


def mix(matrix, parts):
    out = dot_nn(parts_of(jnp.concatenate([matrix] * 3, axis=1)), parts)
    return out[2 * K :] + out[K : 2 * K] + out[:K]


def factor(gram):
    row = lax.broadcasted_iota(jnp.int32, (K, K), 0)
    col = lax.broadcasted_iota(jnp.int32, (K, K), 1)
    upper = gram
    inverse = (row == col).astype(F32)
    for j in range(K):
        ratio = upper[:, j : j + 1] / upper[j : j + 1, j : j + 1]
        ratio = jnp.where(row > j, jnp.broadcast_to(ratio, (K, K)), 0.0)
        upper, inverse = upper - ratio * upper[j : j + 1, :], inverse - ratio * inverse[j : j + 1, :]
    diagonal = jnp.sum(jnp.where(row == col, upper, 0.0), axis=1, keepdims=True)
    scale = 1.0 / jnp.sqrt(diagonal)
    return jnp.where(col >= row, upper * scale, 0.0), inverse * scale


def kernel(
    rows_n, cols_n, pb,
    start, tiles, tile_rows, tile_cols, counts, basis, coef,
    f0, f1, f2, fq1, fw, fq2, dh, dl, lext, permt, chunk, piece, fb, sb, rs, rsib, acc,
    ags, agf, agr, rss, rsr, sibs, sibr,
):
    r = lax.axis_index("row")
    c = lax.axis_index("col")
    other = 1 - c
    piece_lanes = pb * BS
    total = float(rows_n * cols_n * piece_lanes)
    row_blocks = cols_n * pb
    row_lanes = row_blocks * BS
    pairs = BS // 2

    barrier = pltpu.get_barrier_semaphore()
    pl.semaphore_signal(barrier, inc=1, device_id={"row": r, "col": other}, device_id_type=MESH)
    for i in range(1, rows_n):
        pl.semaphore_signal(
            barrier, inc=1, device_id={"row": lax.rem(r + i, rows_n), "col": c}, device_id_type=MESH
        )

    lane = lax.broadcasted_iota(jnp.int32, (8, 128), 1)

    def lanes_of(col, row):
        return pl.ds(pl.multiple_of((col * rows_n + row) * piece_lanes, 128), piece_lanes)

    own = lanes_of(c, r)

    for j in range(pb):
        for m in range(K // 2):
            chunk[j * 8 + m : j * 8 + m + 1, :] = start[j : j + 1, m * 128 : (m + 1) * 128]
    for jp in range(pb // 2):
        one = chunk[jp * 16 : jp * 16 + 8, :]
        two = chunk[jp * 16 + 8 : jp * 16 + 16, :]
        piece[jp, pl.ds(0, 8, stride=2), :] = jnp.where(
            lane < 64, one, pltpu.roll(two, 64, 1)
        )
        piece[jp, pl.ds(1, 8, stride=2), :] = jnp.where(
            lane < 64, pltpu.roll(one, 64, 1), two
        )
    f0[:, own] = jnp.concatenate([piece[jp] for jp in range(pb // 2)], axis=1)

    def ag_copy(ref, ph, col, row, send_sem, target_row, target_col):
        return pltpu.make_async_remote_copy(
            src_ref=ref.at[:, lanes_of(col, row)],
            dst_ref=ref.at[:, lanes_of(col, row)],
            send_sem=send_sem,
            recv_sem=agr.at[ph, col, row],
            device_id={"row": target_row, "col": target_col},
            device_id_type=MESH,
        )

    def ag_start(ref, ph):
        for i in range(rows_n - 1, 0, -1):
            ag_copy(ref, ph, c, r, ags.at[ph, i], lax.rem(r + i, rows_n), c).start()
        ag_copy(ref, ph, c, r, ags.at[ph, 0], r, other).start()

    def ag_forward(ref, ph):
        for i in range(1, rows_n):
            source = lax.rem(r + i, rows_n)
            copy = ag_copy(ref, ph, c, source, agf.at[ph, i], r, other)
            copy.wait_recv()
            copy.start()

    def ag_end(ref, ph, first, last):
        for i in range(first, last):
            source = lax.rem(r + i, rows_n)
            ag_copy(ref, ph, other, source, agf.at[ph, i], r, other).wait_recv()

    def ag_drain(ref, ph):
        for i in range(1, rows_n):
            ag_copy(ref, ph, c, r, ags.at[ph, i], lax.rem(r + i, rows_n), c).wait_send()
            ag_copy(ref, ph, c, lax.rem(r + i, rows_n), agf.at[ph, i], r, other).wait_send()
        ag_copy(ref, ph, c, r, ags.at[ph, 0], r, other).wait_send()

    def rs_copy(ph, source, target):
        return pltpu.make_async_remote_copy(
            src_ref=sb.at[ph, target],
            dst_ref=rs.at[ph, source],
            send_sem=rss.at[ph, target],
            recv_sem=rsr.at[ph, source],
            device_id={"row": target, "col": c},
            device_id_type=MESH,
        )

    def half(col):
        return pl.ds(pl.multiple_of(col * piece_lanes, 128), piece_lanes)

    def sib_copy(ph):
        return pltpu.make_async_remote_copy(
            src_ref=fb.at[ph, :, half(other)],
            dst_ref=rsib.at[ph],
            send_sem=sibs.at[ph],
            recv_sem=sibr.at[ph],
            device_id={"row": r, "col": other},
            device_id_type=MESH,
        )

    pl.semaphore_wait(barrier, rows_n)
    ag_start(f0, 0)

    q = lax.broadcasted_iota(jnp.int32, (row_blocks * pairs, row_lanes), 0)
    p = lax.broadcasted_iota(jnp.int32, (row_blocks * pairs, row_lanes), 1)
    place = (q % row_blocks) * BS + (q // row_blocks) * 2
    permt[0] = (p == place).astype(F32).astype(BF16)
    permt[1] = (p == place + 1).astype(F32).astype(BF16)

    slots = tile_rows.shape[1]
    places = rows_n * pb * row_blocks
    tr = tile_rows[...]
    tc = tile_cols[...]
    position = (
        ((tc // (pb * cols_n)) * pb + tc % pb) * row_blocks + (tr - r * row_blocks)
    )
    slot = lax.broadcasted_iota(jnp.int32, (1, slots), 1)
    position = jnp.where(slot < counts[0], position, -1)
    pick = (lax.broadcasted_iota(jnp.int32, (places, slots), 0) == position).astype(F32).astype(BF16)

    def densify(i, carry):
        high, low = split2(tiles[:, pl.ds(pl.multiple_of(i * 256, 256), 256)])
        x = dot_nn(pick, high) + dot_nn(pick, low)
        for j in range(rows_n * pb):
            block = x[j * 8 : (j + 1) * 8]
            high, low = split2(jnp.concatenate([block[:, :128], block[:, 128:]], axis=0))
            at = pl.ds(pl.multiple_of(i * 16, 16), 16)
            dh[at, j * 128 : (j + 1) * 128] = high
            dl[at, j * 128 : (j + 1) * 128] = low
        return carry

    lax.fori_loop(0, pairs // 2, densify, 0)

    def product(ref, ph):
        across = jnp.concatenate([ref[:, lanes_of(i, r)] for i in range(cols_n)], axis=1)
        parts = jnp.concatenate(split3(across), axis=0)
        even = dot_nt(parts, permt[0]).astype(BF16)
        odd = dot_nt(parts, permt[1]).astype(BF16)
        lrow = jnp.concatenate(
            [x[i * K : (i + 1) * K] for i in range(3) for x in (even, odd)], axis=0
        )
        wide = lax.broadcasted_iota(jnp.int32, (K, 128), 1)
        low_half = wide < 64

        group = 4 if rows_n % 4 == 0 else 1

        def back(step, carry):
            first = rows_n - (step + 1) * group
            for g in range(group - 1, -1, -1):
                target = first + g
                at = pl.ds(pl.multiple_of(target * pb * 128, 128), pb * 128)
                v = ref[:, lanes_of(c, target)]
                extended = []
                for jp in range(pb // 2):
                    x = v[:, jp * 128 : (jp + 1) * 128]
                    y = pltpu.roll(x, 64, 1)
                    extended.append(
                        jnp.concatenate([jnp.where(low_half, x, 0.0), jnp.where(low_half, 0.0, y)], axis=0)
                    )
                    extended.append(
                        jnp.concatenate([jnp.where(low_half, y, 0.0), jnp.where(low_half, 0.0, x)], axis=0)
                    )
                lext[:, at] = jnp.concatenate(split3(jnp.concatenate(extended, axis=1)), axis=0)
                x = dot_nn(lrow, dh[:, at])
                y = dot_nn(lrow[: 4 * K], dl[:, at])
                z = x[4 * K :] + (x[2 * K : 4 * K] + y[2 * K :]) + y[: 2 * K] + x[: 2 * K]
                sums = []
                for j in range(pb):
                    t = jnp.where(
                        low_half, z[:K, j * 128 : (j + 1) * 128], z[K:, j * 128 : (j + 1) * 128]
                    )
                    sums.append(t + pltpu.roll(t, 64, 1))
                sb[ph, target] = jnp.concatenate(
                    [jnp.where(low_half, sums[2 * j], sums[2 * j + 1]) for j in range(pb // 2)], axis=1
                )
            for g in range(group - 1, -1, -1):
                target = first + g

                @pl.when(target > r)
                def _():
                    rs_copy(ph, r, target).start()

            return carry

        lax.fori_loop(0, rows_n // group, back, 0)

        x = dot_nt(dh[...], lext[...]).T
        y = dot_nt(dl[...], lext[: 4 * K, :]).T
        z = x[4 * K :] + (x[2 * K : 4 * K] + y[2 * K :]) + y[: 2 * K] + x[: 2 * K]
        parts = split3(z)
        out = dot_nn(jnp.concatenate([x[:K] for x in parts], axis=0), permt[0]) + dot_nn(
            jnp.concatenate([x[K:] for x in parts], axis=0), permt[1]
        )
        fb[ph] = out[2 * K :] + out[K : 2 * K] + out[:K]
        sib_copy(ph).start()

    def collect(ph):
        acc[...] = sb[ph, r] + fb[ph, :, half(c)]

        def add(source, carry):
            @pl.when(source < r)
            def _():
                rs_copy(ph, source, r).wait_recv()
                acc[...] += rs[ph, source]

            return carry

        lax.fori_loop(0, rows_n, add, 0)
        sib_copy(ph).wait_recv()
        return acc[...] + rsib[ph]

    def rs_drain(ph):
        def step(target, carry):
            @pl.when(target > r)
            def _():
                rs_copy(ph, r, target).wait_send()

            return carry

        lax.fori_loop(0, rows_n, step, 0)
        sib_copy(ph).wait_send()

    identity = (
        lax.broadcasted_iota(jnp.int32, (K, K), 0) == lax.broadcasted_iota(jnp.int32, (K, K), 1)
    ).astype(F32)

    ag_forward(f0, 0)
    ag_end(f0, 0, 0, 1)
    product(f0, 0)
    ag_end(f0, 0, 1, rows_n)
    v = parts_of(f0[...])
    unused, inverse0 = factor(gram_of(v, v) / total)
    fq1[...] = mix(inverse0, v)

    f1[:, own] = collect(0)
    ag_start(f1, 1)
    ag_forward(f1, 1)
    ag_end(f1, 1, 0, 1)
    product(f1, 1)
    ag_end(f1, 1, 1, rows_n)
    z1 = mix(inverse0, parts_of(f1[...]))
    fw[...] = z1
    q1 = parts_of(fq1[...])
    a1 = gram_of(q1, parts_of(z1)) / total
    coef[0] = a1
    a1t = a1.T
    w1 = parts_of(z1 - mix(a1t, q1))
    upper1, inverse1 = factor(gram_of(w1, w1) / total)
    coef[1] = dot_nt(identity, upper1)
    fq2[...] = mix(inverse1, w1)
    behind = mix(inverse1, parts_of(mix(a1t, parts_of(fw[:, own])))) + mix(
        upper1, parts_of(fq1[:, own])
    )
    forward = dot_nn(inverse1, inverse0)

    f2[:, own] = mix(forward, parts_of(collect(1))) - behind
    ag_start(f2, 2)
    ag_forward(f2, 2)
    ag_end(f2, 2, 0, rows_n)
    z2 = f2[...]
    q2 = parts_of(fq2[...])
    a2 = gram_of(q2, parts_of(z2)) / total
    coef[2] = a2
    w2 = z2 - mix(a2.T, q2)
    fw[...] = w2
    w2 = parts_of(w2)
    upper2, inverse2 = factor(gram_of(w2, w2) / total)
    coef[3] = dot_nt(identity, upper2)
    piece_out = mix(inverse2, parts_of(fw[:, own]))
    for jp in range(pb // 2):
        piece[jp] = piece_out[:, jp * 128 : (jp + 1) * 128]
    for jp in range(pb // 2):
        one = piece[jp, pl.ds(0, 8, stride=2), :]
        two = piece[jp, pl.ds(1, 8, stride=2), :]
        chunk[jp * 16 : jp * 16 + 8, :] = jnp.where(lane < 64, one, pltpu.roll(two, 64, 1))
        chunk[jp * 16 + 8 : jp * 16 + 16, :] = jnp.where(lane < 64, pltpu.roll(one, 64, 1), two)
    for j in range(pb):
        for m in range(K // 2):
            basis[j : j + 1, m * 128 : (m + 1) * 128] = chunk[j * 8 + m : j * 8 + m + 1, :]

    for ph, ref in enumerate((f0, f1, f2)):
        ag_drain(ref, ph)
    for ph in range(2):
        rs_drain(ph)


def solution(mesh):
    rows_n = mesh.shape["row"]
    cols_n = mesh.shape["col"]

    def per_device(start_block, tiles, tile_rows, tile_cols, counts):
        pb = start_block.shape[0]
        slots = tile_rows.shape[0]
        length = rows_n * cols_n * pb * BS
        wide = rows_n * pb * 128
        tall = cols_n * pb * BS // 2
        vmem = pl.BlockSpec(memory_space=pltpu.VMEM)
        return pl.pallas_call(
            functools.partial(kernel, rows_n, cols_n, pb),
            out_shape=(
                jax.ShapeDtypeStruct(start_block.shape, F32),
                jax.ShapeDtypeStruct((4, K, K), F32),
            ),
            in_specs=[vmem] * 4 + [pl.BlockSpec(memory_space=pltpu.SMEM)],
            out_specs=(vmem, vmem),
            scratch_shapes=[pltpu.VMEM((K, length), F32)] * 6
            + [
                pltpu.VMEM((tall, wide), BF16),
                pltpu.VMEM((tall, wide), BF16),
                pltpu.VMEM((6 * K, wide), BF16),
                pltpu.VMEM((2, tall, 2 * tall), BF16),
                pltpu.VMEM((pb * K // 2, 128), F32),
                pltpu.VMEM((pb // 2, K, 128), F32),
                pltpu.VMEM((2, K, cols_n * pb * BS), F32),
                pltpu.VMEM((2, rows_n, K, pb * BS), F32),
                pltpu.VMEM((2, rows_n, K, pb * BS), F32),
                pltpu.VMEM((2, K, pb * BS), F32),
                pltpu.VMEM((K, pb * BS), F32),
                pltpu.SemaphoreType.DMA((3, rows_n)),
                pltpu.SemaphoreType.DMA((3, rows_n)),
                pltpu.SemaphoreType.DMA((3, cols_n, rows_n)),
                pltpu.SemaphoreType.DMA((2, rows_n)),
                pltpu.SemaphoreType.DMA((2, rows_n)),
                pltpu.SemaphoreType.DMA((2,)),
                pltpu.SemaphoreType.DMA((2,)),
            ],
            compiler_params=pltpu.CompilerParams(
                collective_id=0, has_side_effects=True, vmem_limit_bytes=56 * 2**20
            ),
        )(
            start_block,
            tiles,
            tile_rows.reshape(1, slots),
            tile_cols.reshape(1, slots),
            counts,
        )

    return jax.shard_map(
        per_device,
        mesh=mesh,
        in_specs=(
            P(("grp", "row", "col"), None),
            P(("grp", "row", "col"), None),
            P(("grp", "row", "col")),
            P(("grp", "row", "col")),
            P(("grp", "row", "col")),
        ),
        out_specs=(P(("grp", "row", "col"), None), P("grp", None, None)),
        check_vma=False,
    )
```

```python
import functools

import jax
import jax.numpy as jnp
from jax import lax
from jax.experimental import pallas as pl
from jax.experimental.pallas import tpu as pltpu
from jax.sharding import PartitionSpec as P

BS = 64
K = 16
F32 = jnp.float32
BF16 = jnp.bfloat16
MESH = pl.DeviceIdType.MESH
HIGHEST = lax.Precision.HIGHEST


def dot_nn(a, b):
    precision = HIGHEST if a.dtype == F32 else None
    return lax.dot_general(a, b, (((1,), (0,)), ((), ())), precision=precision, preferred_element_type=F32)


def dot_nt(a, b):
    precision = HIGHEST if a.dtype == F32 else None
    return lax.dot_general(a, b, (((1,), (1,)), ((), ())), precision=precision, preferred_element_type=F32)


def split2(x):
    high = x.astype(BF16)
    return high, (x - high.astype(F32)).astype(BF16)


def split3(x):
    high = x.astype(BF16)
    rest = x - high.astype(F32)
    middle = rest.astype(BF16)
    return high, middle, (rest - middle.astype(F32)).astype(BF16)


def parts_of(x):
    return jnp.concatenate(split3(x), axis=0)


def gram_of(left, right):
    m = dot_nt(left, right)
    m = m[2 * K :] + m[K : 2 * K] + m[:K]
    return m[:, 2 * K :] + m[:, K : 2 * K] + m[:, :K]


def mix(matrix, parts):
    out = dot_nn(parts_of(jnp.concatenate([matrix] * 3, axis=1)), parts)
    return out[2 * K :] + out[K : 2 * K] + out[:K]


def factor(gram):
    row = lax.broadcasted_iota(jnp.int32, (K, K), 0)
    col = lax.broadcasted_iota(jnp.int32, (K, K), 1)
    upper = gram
    inverse = (row == col).astype(F32)
    columns = [jnp.broadcast_to(gram[:, j : j + 1], (K, K)) for j in range(K)]
    for j in range(K):
        ratio = jnp.where(row > j, columns[j] * (1.0 / columns[j][j : j + 1, :]), 0.0)
        for k in range(j + 1, K):
            columns[k] = columns[k] - ratio * columns[k][j : j + 1, :]
        upper, inverse = upper - ratio * upper[j : j + 1, :], inverse - ratio * inverse[j : j + 1, :]
    diagonal = jnp.sum(jnp.where(row == col, upper, 0.0), axis=1, keepdims=True)
    scale = 1.0 / jnp.sqrt(diagonal)
    return jnp.where(col >= row, upper * scale, 0.0), inverse * scale


def kernel(
    rows_n, cols_n, pb,
    start, tiles_hbm, tile_rows, tile_cols, counts, basis, coef,
    f0, f1, f2, fq1, fw, fq2, dh, dl, lext, permt, chunk, piece, fb, sb, rs, rsib, acc,
    tiles, ags, agf, agr, rss, rsr, sibs, sibr, load,
):
    r = lax.axis_index("row")
    c = lax.axis_index("col")
    other = 1 - c
    piece_lanes = pb * BS
    total = float(rows_n * cols_n * piece_lanes)
    row_blocks = cols_n * pb
    row_lanes = row_blocks * BS
    pairs = BS // 2

    barrier = pltpu.get_barrier_semaphore()
    pl.semaphore_signal(barrier, inc=1, device_id={"row": r, "col": other}, device_id_type=MESH)
    for i in range(1, rows_n):
        pl.semaphore_signal(
            barrier, inc=1, device_id={"row": lax.rem(r + i, rows_n), "col": c}, device_id_type=MESH
        )

    loading = pltpu.make_async_copy(tiles_hbm, tiles, load)
    loading.start()
    lane = lax.broadcasted_iota(jnp.int32, (8, 128), 1)

    def lanes_of(col, row):
        return pl.ds(pl.multiple_of((col * rows_n + row) * piece_lanes, 128), piece_lanes)

    own = lanes_of(c, r)

    for j in range(pb):
        for m in range(K // 2):
            chunk[j * 8 + m : j * 8 + m + 1, :] = start[j : j + 1, m * 128 : (m + 1) * 128]
    for jp in range(pb // 2):
        one = chunk[jp * 16 : jp * 16 + 8, :]
        two = chunk[jp * 16 + 8 : jp * 16 + 16, :]
        piece[jp, pl.ds(0, 8, stride=2), :] = jnp.where(
            lane < 64, one, pltpu.roll(two, 64, 1)
        )
        piece[jp, pl.ds(1, 8, stride=2), :] = jnp.where(
            lane < 64, pltpu.roll(one, 64, 1), two
        )
    f0[:, own] = jnp.concatenate([piece[jp] for jp in range(pb // 2)], axis=1)

    def ag_copy(ref, ph, col, row, send_sem, target_row, target_col):
        return pltpu.make_async_remote_copy(
            src_ref=ref.at[:, lanes_of(col, row)],
            dst_ref=ref.at[:, lanes_of(col, row)],
            send_sem=send_sem,
            recv_sem=agr.at[ph, col, row],
            device_id={"row": target_row, "col": target_col},
            device_id_type=MESH,
        )

    def ag_start(ref, ph):
        for i in range(rows_n - 1, 0, -1):
            ag_copy(ref, ph, c, r, ags.at[ph, i], lax.rem(r + i, rows_n), c).start()
        ag_copy(ref, ph, c, r, ags.at[ph, 0], r, other).start()

    def ag_forward(ref, ph):
        for i in range(1, rows_n):
            source = lax.rem(r + i, rows_n)
            copy = ag_copy(ref, ph, c, source, agf.at[ph, i], r, other)
            copy.wait_recv()
            copy.start()

    def ag_end(ref, ph, first, last):
        for i in range(first, last):
            source = lax.rem(r + i, rows_n)
            ag_copy(ref, ph, other, source, agf.at[ph, i], r, other).wait_recv()

    def ag_drain(ref, ph):
        for i in range(1, rows_n):
            ag_copy(ref, ph, c, r, ags.at[ph, i], lax.rem(r + i, rows_n), c).wait_send()
            ag_copy(ref, ph, c, lax.rem(r + i, rows_n), agf.at[ph, i], r, other).wait_send()
        ag_copy(ref, ph, c, r, ags.at[ph, 0], r, other).wait_send()

    def rs_copy(ph, source, target):
        return pltpu.make_async_remote_copy(
            src_ref=sb.at[ph, target],
            dst_ref=rs.at[ph, source],
            send_sem=rss.at[ph, target],
            recv_sem=rsr.at[ph, source],
            device_id={"row": target, "col": c},
            device_id_type=MESH,
        )

    def half(col):
        return pl.ds(pl.multiple_of(col * piece_lanes, 128), piece_lanes)

    def sib_copy(ph):
        return pltpu.make_async_remote_copy(
            src_ref=fb.at[ph, :, half(other)],
            dst_ref=rsib.at[ph],
            send_sem=sibs.at[ph],
            recv_sem=sibr.at[ph],
            device_id={"row": r, "col": other},
            device_id_type=MESH,
        )

    pl.semaphore_wait(barrier, rows_n)
    ag_start(f0, 0)

    q = lax.broadcasted_iota(jnp.int32, (row_blocks * pairs, row_lanes), 0)
    p = lax.broadcasted_iota(jnp.int32, (row_blocks * pairs, row_lanes), 1)
    place = (q % row_blocks) * BS + (q // row_blocks) * 2
    permt[0] = (p == place).astype(F32).astype(BF16)
    permt[1] = (p == place + 1).astype(F32).astype(BF16)

    slots = tile_rows.shape[1]
    places = rows_n * pb * row_blocks
    tr = tile_rows[...]
    tc = tile_cols[...]
    position = (
        ((tc // (pb * cols_n)) * pb + tc % pb) * row_blocks + (tr - r * row_blocks)
    )
    slot = lax.broadcasted_iota(jnp.int32, (1, slots), 1)
    position = jnp.where(slot < counts[0], position, -1)
    pick = (lax.broadcasted_iota(jnp.int32, (places, slots), 0) == position).astype(F32).astype(BF16)

    def densify(i, carry):
        high, low = split2(tiles[:, pl.ds(pl.multiple_of(i * 256, 256), 256)])
        x = dot_nn(pick, high) + dot_nn(pick, low)
        for j in range(rows_n * pb):
            block = x[j * 8 : (j + 1) * 8]
            high, low = split2(jnp.concatenate([block[:, :128], block[:, 128:]], axis=0))
            at = pl.ds(pl.multiple_of(i * 16, 16), 16)
            dh[at, j * 128 : (j + 1) * 128] = high
            dl[at, j * 128 : (j + 1) * 128] = low
        return carry

    loading.wait()
    lax.fori_loop(0, pairs // 2, densify, 0)

    def product(ref, ph):
        across = jnp.concatenate([ref[:, lanes_of(i, r)] for i in range(cols_n)], axis=1)
        parts = jnp.concatenate(split3(across), axis=0)
        even = dot_nt(parts, permt[0]).astype(BF16)
        odd = dot_nt(parts, permt[1]).astype(BF16)
        lrow = jnp.concatenate(
            [x[i * K : (i + 1) * K] for i in range(3) for x in (even, odd)], axis=0
        )
        wide = lax.broadcasted_iota(jnp.int32, (K, 128), 1)
        low_half = wide < 64

        group = 4 if rows_n % 4 == 0 else 1

        def back(step, carry):
            first = rows_n - (step + 1) * group
            for g in range(group - 1, -1, -1):
                target = first + g
                at = pl.ds(pl.multiple_of(target * pb * 128, 128), pb * 128)
                v = ref[:, lanes_of(c, target)]
                extended = []
                for jp in range(pb // 2):
                    x = v[:, jp * 128 : (jp + 1) * 128]
                    y = pltpu.roll(x, 64, 1)
                    extended.append(
                        jnp.concatenate([jnp.where(low_half, x, 0.0), jnp.where(low_half, 0.0, y)], axis=0)
                    )
                    extended.append(
                        jnp.concatenate([jnp.where(low_half, y, 0.0), jnp.where(low_half, 0.0, x)], axis=0)
                    )
                lext[:, at] = jnp.concatenate(split3(jnp.concatenate(extended, axis=1)), axis=0)
                x = dot_nn(lrow, dh[:, at])
                y = dot_nn(lrow[: 4 * K], dl[:, at])
                z = x[4 * K :] + (x[2 * K : 4 * K] + y[2 * K :]) + y[: 2 * K] + x[: 2 * K]
                sums = []
                for j in range(pb):
                    t = jnp.where(
                        low_half, z[:K, j * 128 : (j + 1) * 128], z[K:, j * 128 : (j + 1) * 128]
                    )
                    sums.append(t + pltpu.roll(t, 64, 1))
                sb[ph, target] = jnp.concatenate(
                    [jnp.where(low_half, sums[2 * j], sums[2 * j + 1]) for j in range(pb // 2)], axis=1
                )
            for g in range(group - 1, -1, -1):
                target = first + g

                @pl.when(target > r)
                def _():
                    rs_copy(ph, r, target).start()

            return carry

        lax.fori_loop(0, rows_n // group, back, 0)

        x = dot_nt(dh[...], lext[...]).T
        y = dot_nt(dl[...], lext[: 4 * K, :]).T
        z = x[4 * K :] + (x[2 * K : 4 * K] + y[2 * K :]) + y[: 2 * K] + x[: 2 * K]
        parts = split3(z)
        out = dot_nn(jnp.concatenate([x[:K] for x in parts], axis=0), permt[0]) + dot_nn(
            jnp.concatenate([x[K:] for x in parts], axis=0), permt[1]
        )
        fb[ph] = out[2 * K :] + out[K : 2 * K] + out[:K]
        sib_copy(ph).start()

    def collect(ph):
        acc[...] = sb[ph, r] + fb[ph, :, half(c)]

        def add(source, carry):
            @pl.when(source < r)
            def _():
                rs_copy(ph, source, r).wait_recv()
                acc[...] += rs[ph, source]

            return carry

        lax.fori_loop(0, rows_n, add, 0)
        sib_copy(ph).wait_recv()
        return acc[...] + rsib[ph]

    def rs_drain(ph):
        def step(target, carry):
            @pl.when(target > r)
            def _():
                rs_copy(ph, r, target).wait_send()

            return carry

        lax.fori_loop(0, rows_n, step, 0)
        sib_copy(ph).wait_send()

    identity = (
        lax.broadcasted_iota(jnp.int32, (K, K), 0) == lax.broadcasted_iota(jnp.int32, (K, K), 1)
    ).astype(F32)

    ag_forward(f0, 0)
    ag_end(f0, 0, 0, 1)
    product(f0, 0)
    ag_end(f0, 0, 1, rows_n)
    v = parts_of(f0[...])
    unused, inverse0 = factor(gram_of(v, v) / total)
    fq1[...] = mix(inverse0, v)

    f1[:, own] = collect(0)
    ag_start(f1, 1)
    ag_forward(f1, 1)
    ag_end(f1, 1, 0, 1)
    product(f1, 1)
    ag_end(f1, 1, 1, rows_n)
    z1 = mix(inverse0, parts_of(f1[...]))
    fw[...] = z1
    q1 = parts_of(fq1[...])
    a1 = gram_of(q1, parts_of(z1)) / total
    coef[0] = a1
    a1t = a1.T
    w1 = parts_of(z1 - mix(a1t, q1))
    upper1, inverse1 = factor(gram_of(w1, w1) / total)
    coef[1] = dot_nt(identity, upper1)
    fq2[...] = mix(inverse1, w1)
    behind = mix(inverse1, parts_of(mix(a1t, parts_of(fw[:, own])))) + mix(
        upper1, parts_of(fq1[:, own])
    )
    forward = dot_nn(inverse1, inverse0)

    f2[:, own] = mix(forward, parts_of(collect(1))) - behind
    ag_start(f2, 2)
    ag_forward(f2, 2)
    ag_end(f2, 2, 0, rows_n)
    z2 = f2[...]
    q2 = parts_of(fq2[...])
    a2 = gram_of(q2, parts_of(z2)) / total
    coef[2] = a2
    w2 = z2 - mix(a2.T, q2)
    fw[...] = w2
    w2 = parts_of(w2)
    upper2, inverse2 = factor(gram_of(w2, w2) / total)
    coef[3] = dot_nt(identity, upper2)
    piece_out = mix(inverse2, parts_of(fw[:, own]))
    for jp in range(pb // 2):
        piece[jp] = piece_out[:, jp * 128 : (jp + 1) * 128]
    for jp in range(pb // 2):
        one = piece[jp, pl.ds(0, 8, stride=2), :]
        two = piece[jp, pl.ds(1, 8, stride=2), :]
        chunk[jp * 16 : jp * 16 + 8, :] = jnp.where(lane < 64, one, pltpu.roll(two, 64, 1))
        chunk[jp * 16 + 8 : jp * 16 + 16, :] = jnp.where(lane < 64, pltpu.roll(one, 64, 1), two)
    for j in range(pb):
        for m in range(K // 2):
            basis[j : j + 1, m * 128 : (m + 1) * 128] = chunk[j * 8 + m : j * 8 + m + 1, :]

    for ph, ref in enumerate((f0, f1, f2)):
        ag_drain(ref, ph)
    for ph in range(2):
        rs_drain(ph)


def store_both(basis, coef, basis_out, coef_out):
    basis_out[...] = basis[...]
    coef_out[...] = coef[...]


def solution(mesh):
    rows_n = mesh.shape["row"]
    cols_n = mesh.shape["col"]

    def per_device(start_block, tiles, tile_rows, tile_cols, counts):
        pb = start_block.shape[0]
        slots = tile_rows.shape[0]
        length = rows_n * cols_n * pb * BS
        wide = rows_n * pb * 128
        tall = cols_n * pb * BS // 2
        vmem = pl.BlockSpec(memory_space=pltpu.VMEM)
        results = pl.pallas_call(
            functools.partial(kernel, rows_n, cols_n, pb),
            out_shape=(
                jax.ShapeDtypeStruct(start_block.shape, F32),
                jax.ShapeDtypeStruct((4, K, K), F32),
            ),
            in_specs=[vmem, pl.BlockSpec(memory_space=pl.ANY), vmem, vmem, pl.BlockSpec(memory_space=pltpu.SMEM)],
            out_specs=(vmem, vmem),
            scratch_shapes=[pltpu.VMEM((K, length), F32)] * 6
            + [
                pltpu.VMEM((tall, wide), BF16),
                pltpu.VMEM((tall, wide), BF16),
                pltpu.VMEM((6 * K, wide), BF16),
                pltpu.VMEM((2, tall, 2 * tall), BF16),
                pltpu.VMEM((pb * K // 2, 128), F32),
                pltpu.VMEM((pb // 2, K, 128), F32),
                pltpu.VMEM((2, K, cols_n * pb * BS), F32),
                pltpu.VMEM((2, rows_n, K, pb * BS), F32),
                pltpu.VMEM((2, rows_n, K, pb * BS), F32),
                pltpu.VMEM((2, K, pb * BS), F32),
                pltpu.VMEM((K, pb * BS), F32),
                pltpu.VMEM(tiles.shape, F32),
                pltpu.SemaphoreType.DMA((3, rows_n)),
                pltpu.SemaphoreType.DMA((3, rows_n)),
                pltpu.SemaphoreType.DMA((3, cols_n, rows_n)),
                pltpu.SemaphoreType.DMA((2, rows_n)),
                pltpu.SemaphoreType.DMA((2, rows_n)),
                pltpu.SemaphoreType.DMA((2,)),
                pltpu.SemaphoreType.DMA((2,)),
                pltpu.SemaphoreType.DMA,
            ],
            compiler_params=pltpu.CompilerParams(
                collective_id=0, has_side_effects=True, vmem_limit_bytes=56 * 2**20
            ),
        )(
            start_block,
            tiles,
            tile_rows.reshape(1, slots),
            tile_cols.reshape(1, slots),
            counts,
        )
        return pl.pallas_call(
            store_both,
            out_shape=tuple(jax.ShapeDtypeStruct(x.shape, F32) for x in results),
            in_specs=[vmem, vmem],
            out_specs=(vmem, vmem),
        )(*results)

    return jax.shard_map(
        per_device,
        mesh=mesh,
        in_specs=(
            P(("grp", "row", "col"), None),
            P(("grp", "row", "col"), None),
            P(("grp", "row", "col")),
            P(("grp", "row", "col")),
            P(("grp", "row", "col")),
        ),
        out_specs=(P(("grp", "row", "col"), None), P("grp", None, None)),
        check_vma=False,
    )
```

```python
import functools

import jax
import jax.numpy as jnp
from jax import lax
from jax.experimental import pallas as pl
from jax.experimental.pallas import tpu as pltpu
from jax.sharding import PartitionSpec as P

BS = 64
K = 16
F32 = jnp.float32
BF16 = jnp.bfloat16
MESH = pl.DeviceIdType.MESH
HIGHEST = lax.Precision.HIGHEST


def dot_nn(a, b):
    precision = HIGHEST if a.dtype == F32 else None
    return lax.dot_general(a, b, (((1,), (0,)), ((), ())), precision=precision, preferred_element_type=F32)


def dot_nt(a, b):
    precision = HIGHEST if a.dtype == F32 else None
    return lax.dot_general(a, b, (((1,), (1,)), ((), ())), precision=precision, preferred_element_type=F32)


def split2(x):
    high = x.astype(BF16)
    return high, (x - high.astype(F32)).astype(BF16)


def split3(x):
    high = x.astype(BF16)
    rest = x - high.astype(F32)
    middle = rest.astype(BF16)
    return high, middle, (rest - middle.astype(F32)).astype(BF16)


def parts_of(x):
    return jnp.concatenate(split3(x), axis=0)


def gram_of(left, right):
    m = dot_nt(left, right)
    m = m[2 * K :] + m[K : 2 * K] + m[:K]
    return m[:, 2 * K :] + m[:, K : 2 * K] + m[:, :K]


def mix(matrix, parts):
    out = dot_nn(parts_of(jnp.concatenate([matrix] * 3, axis=1)), parts)
    return out[2 * K :] + out[K : 2 * K] + out[:K]


def factor(gram):
    row = lax.broadcasted_iota(jnp.int32, (K, K), 0)
    col = lax.broadcasted_iota(jnp.int32, (K, K), 1)
    upper = gram
    inverse = (row == col).astype(F32)
    columns = [jnp.broadcast_to(gram[:, j : j + 1], (K, K)) for j in range(K)]
    for j in range(K):
        ratio = jnp.where(row > j, columns[j] * (1.0 / columns[j][j : j + 1, :]), 0.0)
        for k in range(j + 1, K):
            columns[k] = columns[k] - ratio * columns[k][j : j + 1, :]
        upper, inverse = upper - ratio * upper[j : j + 1, :], inverse - ratio * inverse[j : j + 1, :]
    diagonal = jnp.sum(jnp.where(row == col, upper, 0.0), axis=1, keepdims=True)
    scale = 1.0 / jnp.sqrt(diagonal)
    return jnp.where(col >= row, upper * scale, 0.0), inverse * scale


def kernel(
    rows_n, cols_n, pb,
    start, tiles_hbm, tile_rows, tile_cols, counts, basis, coef,
    f0, f1, f2, fq1, fw, fq2, dh, dl, lext, permt, chunk, piece, fb, sb, rs, rsib, acc,
    tiles, ags, agf, agr, rss, rsr, sibs, sibr, load,
):
    r = lax.axis_index("row")
    c = lax.axis_index("col")
    other = 1 - c
    piece_lanes = pb * BS
    total = float(rows_n * cols_n * piece_lanes)
    row_blocks = cols_n * pb
    row_lanes = row_blocks * BS
    pairs = BS // 2

    barrier = pltpu.get_barrier_semaphore()
    pl.semaphore_signal(barrier, inc=1, device_id={"row": r, "col": other}, device_id_type=MESH)
    for i in range(1, rows_n):
        pl.semaphore_signal(
            barrier, inc=1, device_id={"row": lax.rem(r + i, rows_n), "col": c}, device_id_type=MESH
        )

    loading = pltpu.make_async_copy(tiles_hbm, tiles, load)
    loading.start()
    lane = lax.broadcasted_iota(jnp.int32, (8, 128), 1)

    def lanes_of(col, row):
        return pl.ds(pl.multiple_of((col * rows_n + row) * piece_lanes, 128), piece_lanes)

    own = lanes_of(c, r)

    for j in range(pb):
        for m in range(K // 2):
            chunk[j * 8 + m : j * 8 + m + 1, :] = start[j : j + 1, m * 128 : (m + 1) * 128]
    for jp in range(pb // 2):
        one = chunk[jp * 16 : jp * 16 + 8, :]
        two = chunk[jp * 16 + 8 : jp * 16 + 16, :]
        piece[jp, pl.ds(0, 8, stride=2), :] = jnp.where(
            lane < 64, one, pltpu.roll(two, 64, 1)
        )
        piece[jp, pl.ds(1, 8, stride=2), :] = jnp.where(
            lane < 64, pltpu.roll(one, 64, 1), two
        )
    f0[:, own] = jnp.concatenate([piece[jp] for jp in range(pb // 2)], axis=1)

    def ag_copy(ref, ph, col, row, send_sem, target_row, target_col):
        return pltpu.make_async_remote_copy(
            src_ref=ref.at[:, lanes_of(col, row)],
            dst_ref=ref.at[:, lanes_of(col, row)],
            send_sem=send_sem,
            recv_sem=agr.at[ph, col, row],
            device_id={"row": target_row, "col": target_col},
            device_id_type=MESH,
        )

    def ag_start(ref, ph):
        for i in range(rows_n - 1, 0, -1):
            ag_copy(ref, ph, c, r, ags.at[ph, i], lax.rem(r + i, rows_n), c).start()
        ag_copy(ref, ph, c, r, ags.at[ph, 0], r, other).start()

    def ag_forward(ref, ph):
        for i in range(1, rows_n):
            source = lax.rem(r + i, rows_n)
            copy = ag_copy(ref, ph, c, source, agf.at[ph, i], r, other)
            copy.wait_recv()
            copy.start()

    def ag_end(ref, ph, first, last):
        for i in range(first, last):
            source = lax.rem(r + i, rows_n)
            ag_copy(ref, ph, other, source, agf.at[ph, i], r, other).wait_recv()

    def ag_drain(ref, ph):
        for i in range(1, rows_n):
            ag_copy(ref, ph, c, r, ags.at[ph, i], lax.rem(r + i, rows_n), c).wait_send()
            ag_copy(ref, ph, c, lax.rem(r + i, rows_n), agf.at[ph, i], r, other).wait_send()
        ag_copy(ref, ph, c, r, ags.at[ph, 0], r, other).wait_send()

    def rs_copy(ph, source, target):
        return pltpu.make_async_remote_copy(
            src_ref=sb.at[ph, target],
            dst_ref=rs.at[ph, source],
            send_sem=rss.at[ph, target],
            recv_sem=rsr.at[ph, source],
            device_id={"row": target, "col": c},
            device_id_type=MESH,
        )

    def half(col):
        return pl.ds(pl.multiple_of(col * piece_lanes, 128), piece_lanes)

    def sib_copy(ph):
        return pltpu.make_async_remote_copy(
            src_ref=fb.at[ph, :, half(other)],
            dst_ref=rsib.at[ph],
            send_sem=sibs.at[ph],
            recv_sem=sibr.at[ph],
            device_id={"row": r, "col": other},
            device_id_type=MESH,
        )

    pl.semaphore_wait(barrier, rows_n)
    ag_start(f0, 0)

    q = lax.broadcasted_iota(jnp.int32, (row_blocks * pairs, row_lanes), 0)
    p = lax.broadcasted_iota(jnp.int32, (row_blocks * pairs, row_lanes), 1)
    place = (q % row_blocks) * BS + (q // row_blocks) * 2
    permt[0] = (p == place).astype(F32).astype(BF16)
    permt[1] = (p == place + 1).astype(F32).astype(BF16)

    slots = tile_rows.shape[1]
    places = rows_n * pb * row_blocks
    tr = tile_rows[...]
    tc = tile_cols[...]
    position = (
        ((tc // (pb * cols_n)) * pb + tc % pb) * row_blocks + (tr - r * row_blocks)
    )
    slot = lax.broadcasted_iota(jnp.int32, (1, slots), 1)
    position = jnp.where(slot < counts[0], position, -1)
    pick = (lax.broadcasted_iota(jnp.int32, (places, slots), 0) == position).astype(F32).astype(BF16)

    def densify(i, carry):
        high, low = split2(tiles[:, pl.ds(pl.multiple_of(i * 256, 256), 256)])
        x = dot_nn(pick, high) + dot_nn(pick, low)
        for j in range(rows_n * pb):
            block = x[j * 8 : (j + 1) * 8]
            high, low = split2(jnp.concatenate([block[:, :128], block[:, 128:]], axis=0))
            at = pl.ds(pl.multiple_of(i * 16, 16), 16)
            dh[at, j * 128 : (j + 1) * 128] = high
            dl[at, j * 128 : (j + 1) * 128] = low
        return carry

    loading.wait()
    lax.fori_loop(0, pairs // 2, densify, 0)

    wide = lax.broadcasted_iota(jnp.int32, (K, 128), 1)
    low_half = wide < 64
    group = 4 if rows_n % 4 == 0 else 1

    def back_product(ref, ph):
        across = jnp.concatenate([ref[:, lanes_of(i, r)] for i in range(cols_n)], axis=1)
        parts = jnp.concatenate(split3(across), axis=0)
        even = dot_nt(parts, permt[0]).astype(BF16)
        odd = dot_nt(parts, permt[1]).astype(BF16)
        lrow = jnp.concatenate(
            [x[i * K : (i + 1) * K] for i in range(3) for x in (even, odd)], axis=0
        )
        def back(step, carry):
            first = rows_n - (step + 1) * group
            for g in range(group - 1, -1, -1):
                target = first + g
                at = pl.ds(pl.multiple_of(target * pb * 128, 128), pb * 128)
                x = dot_nn(lrow, dh[:, at])
                y = dot_nn(lrow[: 4 * K], dl[:, at])
                z = x[4 * K :] + (x[2 * K : 4 * K] + y[2 * K :]) + y[: 2 * K] + x[: 2 * K]
                sums = []
                for j in range(pb):
                    t = jnp.where(
                        low_half, z[:K, j * 128 : (j + 1) * 128], z[K:, j * 128 : (j + 1) * 128]
                    )
                    sums.append(t + pltpu.roll(t, 64, 1))
                sb[ph, target] = jnp.concatenate(
                    [jnp.where(low_half, sums[2 * j], sums[2 * j + 1]) for j in range(pb // 2)], axis=1
                )
            for g in range(group - 1, -1, -1):
                target = first + g

                @pl.when(target > r)
                def _():
                    rs_copy(ph, r, target).start()

            return carry

        lax.fori_loop(0, rows_n // group, back, 0)

    def front_product(ref, ph):
        def extend(step, carry):
            for g in range(group):
                target = step * group + g
                at = pl.ds(pl.multiple_of(target * pb * 128, 128), pb * 128)
                v = ref[:, lanes_of(c, target)]
                extended = []
                for jp in range(pb // 2):
                    x = v[:, jp * 128 : (jp + 1) * 128]
                    y = pltpu.roll(x, 64, 1)
                    extended.append(
                        jnp.concatenate([jnp.where(low_half, x, 0.0), jnp.where(low_half, 0.0, y)], axis=0)
                    )
                    extended.append(
                        jnp.concatenate([jnp.where(low_half, y, 0.0), jnp.where(low_half, 0.0, x)], axis=0)
                    )
                lext[:, at] = jnp.concatenate(split3(jnp.concatenate(extended, axis=1)), axis=0)
            return carry

        lax.fori_loop(0, rows_n // group, extend, 0)

        x = dot_nt(dh[...], lext[...]).T
        y = dot_nt(dl[...], lext[: 4 * K, :]).T
        z = x[4 * K :] + (x[2 * K : 4 * K] + y[2 * K :]) + y[: 2 * K] + x[: 2 * K]
        parts = split3(z)
        out = dot_nn(jnp.concatenate([x[:K] for x in parts], axis=0), permt[0]) + dot_nn(
            jnp.concatenate([x[K:] for x in parts], axis=0), permt[1]
        )
        fb[ph] = out[2 * K :] + out[K : 2 * K] + out[:K]
        sib_copy(ph).start()

    def collect(ph):
        acc[...] = sb[ph, r] + fb[ph, :, half(c)]

        def add(source, carry):
            @pl.when(source < r)
            def _():
                rs_copy(ph, source, r).wait_recv()
                acc[...] += rs[ph, source]

            return carry

        lax.fori_loop(0, rows_n, add, 0)
        sib_copy(ph).wait_recv()
        return acc[...] + rsib[ph]

    def rs_drain(ph):
        def step(target, carry):
            @pl.when(target > r)
            def _():
                rs_copy(ph, r, target).wait_send()

            return carry

        lax.fori_loop(0, rows_n, step, 0)
        sib_copy(ph).wait_send()

    identity = (
        lax.broadcasted_iota(jnp.int32, (K, K), 0) == lax.broadcasted_iota(jnp.int32, (K, K), 1)
    ).astype(F32)

    ag_end(f0, 0, 0, 1)
    back_product(f0, 0)
    ag_forward(f0, 0)
    front_product(f0, 0)
    ag_end(f0, 0, 1, rows_n)
    v = parts_of(f0[...])
    unused, inverse0 = factor(gram_of(v, v) / total)
    fq1[...] = mix(inverse0, v)

    f1[:, own] = collect(0)
    ag_start(f1, 1)
    ag_end(f1, 1, 0, 1)
    back_product(f1, 1)
    ag_forward(f1, 1)
    front_product(f1, 1)
    ag_end(f1, 1, 1, rows_n)
    z1 = mix(inverse0, parts_of(f1[...]))
    fw[...] = z1
    q1 = parts_of(fq1[...])
    a1 = gram_of(q1, parts_of(z1)) / total
    coef[0] = a1
    a1t = a1.T
    w1 = parts_of(z1 - mix(a1t, q1))
    upper1, inverse1 = factor(gram_of(w1, w1) / total)
    coef[1] = dot_nt(identity, upper1)
    fq2[...] = mix(inverse1, w1)
    behind = mix(inverse1, parts_of(mix(a1t, parts_of(fw[:, own])))) + mix(
        upper1, parts_of(fq1[:, own])
    )
    forward = dot_nn(inverse1, inverse0)

    f2[:, own] = mix(forward, parts_of(collect(1))) - behind
    ag_start(f2, 2)
    ag_forward(f2, 2)
    ag_end(f2, 2, 0, rows_n)
    z2 = f2[...]
    q2 = parts_of(fq2[...])
    a2 = gram_of(q2, parts_of(z2)) / total
    coef[2] = a2
    w2 = z2 - mix(a2.T, q2)
    fw[...] = w2
    w2 = parts_of(w2)
    upper2, inverse2 = factor(gram_of(w2, w2) / total)
    coef[3] = dot_nt(identity, upper2)
    piece_out = mix(inverse2, parts_of(fw[:, own]))
    for jp in range(pb // 2):
        piece[jp] = piece_out[:, jp * 128 : (jp + 1) * 128]
    for jp in range(pb // 2):
        one = piece[jp, pl.ds(0, 8, stride=2), :]
        two = piece[jp, pl.ds(1, 8, stride=2), :]
        chunk[jp * 16 : jp * 16 + 8, :] = jnp.where(lane < 64, one, pltpu.roll(two, 64, 1))
        chunk[jp * 16 + 8 : jp * 16 + 16, :] = jnp.where(lane < 64, pltpu.roll(one, 64, 1), two)
    for j in range(pb):
        for m in range(K // 2):
            basis[j : j + 1, m * 128 : (m + 1) * 128] = chunk[j * 8 + m : j * 8 + m + 1, :]

    for ph, ref in enumerate((f0, f1, f2)):
        ag_drain(ref, ph)
    for ph in range(2):
        rs_drain(ph)


def store_both(basis, coef, basis_out, coef_out):
    basis_out[...] = basis[...]
    coef_out[...] = coef[...]


def solution(mesh):
    rows_n = mesh.shape["row"]
    cols_n = mesh.shape["col"]

    def per_device(start_block, tiles, tile_rows, tile_cols, counts):
        pb = start_block.shape[0]
        slots = tile_rows.shape[0]
        length = rows_n * cols_n * pb * BS
        wide = rows_n * pb * 128
        tall = cols_n * pb * BS // 2
        vmem = pl.BlockSpec(memory_space=pltpu.VMEM)
        results = pl.pallas_call(
            functools.partial(kernel, rows_n, cols_n, pb),
            out_shape=(
                jax.ShapeDtypeStruct(start_block.shape, F32),
                jax.ShapeDtypeStruct((4, K, K), F32),
            ),
            in_specs=[vmem, pl.BlockSpec(memory_space=pl.ANY), vmem, vmem, pl.BlockSpec(memory_space=pltpu.SMEM)],
            out_specs=(vmem, vmem),
            scratch_shapes=[pltpu.VMEM((K, length), F32)] * 6
            + [
                pltpu.VMEM((tall, wide), BF16),
                pltpu.VMEM((tall, wide), BF16),
                pltpu.VMEM((6 * K, wide), BF16),
                pltpu.VMEM((2, tall, 2 * tall), BF16),
                pltpu.VMEM((pb * K // 2, 128), F32),
                pltpu.VMEM((pb // 2, K, 128), F32),
                pltpu.VMEM((2, K, cols_n * pb * BS), F32),
                pltpu.VMEM((2, rows_n, K, pb * BS), F32),
                pltpu.VMEM((2, rows_n, K, pb * BS), F32),
                pltpu.VMEM((2, K, pb * BS), F32),
                pltpu.VMEM((K, pb * BS), F32),
                pltpu.VMEM(tiles.shape, F32),
                pltpu.SemaphoreType.DMA((3, rows_n)),
                pltpu.SemaphoreType.DMA((3, rows_n)),
                pltpu.SemaphoreType.DMA((3, cols_n, rows_n)),
                pltpu.SemaphoreType.DMA((2, rows_n)),
                pltpu.SemaphoreType.DMA((2, rows_n)),
                pltpu.SemaphoreType.DMA((2,)),
                pltpu.SemaphoreType.DMA((2,)),
                pltpu.SemaphoreType.DMA,
            ],
            compiler_params=pltpu.CompilerParams(
                collective_id=0, has_side_effects=True, vmem_limit_bytes=56 * 2**20
            ),
        )(
            start_block,
            tiles,
            tile_rows.reshape(1, slots),
            tile_cols.reshape(1, slots),
            counts,
        )
        return pl.pallas_call(
            store_both,
            out_shape=tuple(jax.ShapeDtypeStruct(x.shape, F32) for x in results),
            in_specs=[vmem, vmem],
            out_specs=(vmem, vmem),
        )(*results)

    return jax.shard_map(
        per_device,
        mesh=mesh,
        in_specs=(
            P(("grp", "row", "col"), None),
            P(("grp", "row", "col"), None),
            P(("grp", "row", "col")),
            P(("grp", "row", "col")),
            P(("grp", "row", "col")),
        ),
        out_specs=(P(("grp", "row", "col"), None), P("grp", None, None)),
        check_vma=False,
    )
```
